32 devices in a mesh: rad: 4 (over y, x), azi: 8 (over z, core).
Axes of the slice: x: 2, y: 2, z: 4, core: 2. Of those that a mesh axis runs over, the one named last changes fastest.
Arguments:
- fluid_state: float32 [32, 8, 16, 8192], P('rad', None, None, 'azi'), may hold values from -6 to 6
- orbit_shift: int32 [32], P('rad'), may hold values from 0 to 8191
- residual_speed: float32 [32], P('rad'), may hold values from -0.5 to 0.5
- coupling: float32 [8, 8], replicated, may hold values from -1.2 to 1.2
- radial_solve: float32 [8, 32, 32], replicated, as said below
Outputs:
- advanced: float32 [32, 8, 16, 8192], P('rad', None, None, 'azi')
The draws below stay inside these ranges and needn't reach their ends.
Inputs may be any that keep to these rules, and one draw needn't show every extreme that they name: radial_solve is, for each field, a dense block of the inverse of the radial operator over the window's radii, whose entries fall off with the distance of the two radii.
All inputs are finite; a program needn't handle non-finite values.
Results may differ from the reference program's by a relative error of at most 0.0003.
Values sent between devices are 32-bit elements; how exact they have to be, the bound alone decides.
A program may use at most 128 MiB of HBM per device.

```python
import jax
import jax.numpy as jnp
from jax import lax

FIELDS = 8
PLANES = 16
R_DEV = 8
NR = 32
NPHI = 8192


def draw_radial_solve(key, part):
    length = 2.0 * R_DEV
    first = jnp.arange(NR)[:, None]
    second = jnp.arange(NR)[None, :]
    distance = jnp.abs(first - second).astype(jnp.float32)
    identity = (first == second).astype(jnp.float32)
    noise = jax.random.normal(key, (FIELDS, NR, NR), jnp.float32)
    return (identity + noise / jnp.sqrt(length)) * jnp.exp(-distance / length)


def with_ends(result, rng, low, high):
    spot = [jax.random.randint(jax.random.fold_in(rng, axis), (), 0, length) for axis, length in enumerate(result.shape)]
    main_axis = result.shape.index(max(result.shape))
    neighbour = spot[:main_axis] + [(spot[main_axis] + 1) % result.shape[main_axis]] + spot[main_axis + 1:]
    return result.at[tuple(spot)].set(low).at[tuple(neighbour)].set(high)


def block_scale(rng, extent, pieces, least, high):
    def one(dim, parts):
        steps = jax.random.uniform(jax.random.fold_in(jax.random.fold_in(rng, 6), dim), (parts,), jnp.float32, least / len(pieces), high / len(pieces))
        return jnp.repeat(jnp.exp(steps), extent[dim] // parts).reshape((-1,) + (1,) * (len(extent) - dim - 1))

    factor_of = one(*pieces[0])
    for cut in pieces[1:]:
        factor_of = factor_of * one(*cut)
    return factor_of


def bell_draw(key, dims, width, limit, split=(), held_as=jnp.bfloat16):
    entries = width * jax.random.normal(key, dims, jnp.float32)
    if split:
        entries = entries * block_scale(key, dims, split, -0.22, 0.18)
    return jnp.clip(entries, -limit, limit).astype(held_as)


def setup_inputs(seed: int = 0) -> dict:
    keys = jax.random.split(jax.random.key(seed), 6)
    return {
        "fluid_state": bell_draw(keys[0], (NR, FIELDS, PLANES, NPHI), 1.0, 6.0, ((0, 4), (3, 8)), jnp.float32),
        "orbit_shift": with_ends(jax.random.randint(keys[1], (NR,), 0, NPHI), jax.random.fold_in(keys[1], 1), 0, NPHI - 1).astype(jnp.int32),
        "residual_speed": jnp.clip(jax.random.uniform(keys[2], (NR,), jnp.float32, -0.5, 0.5) * block_scale(keys[2], (NR,), ((0, 4),), -0.4, 0.0), -0.5, 0.5),
        "coupling": bell_draw(keys[3], (FIELDS, FIELDS), 0.2, 1.2, (), jnp.float32),
        "radial_solve": draw_radial_solve(jax.random.fold_in(keys[5], 71), 0),
    }


def face_flux(left, right, speed):
    return 0.5 * speed * (left + right) - 0.5 * jnp.abs(speed) * (right - left)


def reference(fluid_state, orbit_shift, residual_speed, coupling, radial_solve):
    columns = jnp.arange(NPHI, dtype=jnp.int32)

    def remap_row(items):
        row, amount = items
        where = jnp.mod(columns - amount, NPHI).astype(jnp.int32)
        return jnp.take(row, where, axis=2)

    remapped = lax.map(remap_row, (fluid_state, orbit_shift))
    speed = residual_speed[:, None, None, None]
    upper = jnp.roll(remapped, -1, axis=3)
    lower = jnp.roll(remapped, 1, axis=3)
    advected = remapped - (face_flux(remapped, upper, speed) - face_flux(lower, remapped, speed))
    padded = jnp.pad(advected, ((1, 1), (0, 0), (0, 0), (0, 0)))
    explicit = advected + jnp.einsum("fg,rgzj->rfzj", coupling, padded[2:] - padded[:-2], precision=lax.Precision.HIGHEST)
    return jnp.einsum("frk,kfzj->rfzj", radial_solve, explicit, precision=lax.Precision.HIGHEST)
```

```python
import jax
import jax.numpy as jnp
from jax import lax
from jax.sharding import PartitionSpec as P


def combined_matrix(coupling, radial_solve):
    fields, radii, _ = radial_solve.shape
    padded = jnp.pad(radial_solve, ((0, 0), (0, 0), (1, 1)))
    differences = padded[:, :, :-2] - padded[:, :, 2:]
    same = jnp.eye(fields, dtype=jnp.float32)
    solve = radial_solve.transpose(1, 0, 2)[:, :, :, None] * same[None, :, None, :]
    mixed = differences.transpose(1, 0, 2)[:, :, :, None] * coupling[None, :, None, :]
    return (solve + mixed).reshape(radii * fields, radii * fields)


def swap_in_plane(value, share):
    blocks = lax.axis_size("azi")
    groups = [list(range(first, first + share)) for first in range(0, blocks, share)]
    return lax.all_to_all(value, "azi", 0, 0, axis_index_groups=groups, tiled=True)


def per_device(fluid_state, orbit_shift, residual_speed, coupling, radial_solve):
    rows, fields, planes, cells = fluid_state.shape
    bands, blocks = lax.axis_size("rad"), lax.axis_size("azi")
    share = bands * blocks // planes
    per = rows // share
    part = lax.axis_index("azi") % share
    cycle = blocks * cells
    matrix = combined_matrix(coupling, radial_solve)
    shifts = lax.all_gather(orbit_shift, "rad").reshape(bands, share, per)
    speeds = lax.all_gather(residual_speed, "rad").reshape(bands, share, per)
    shifts = lax.dynamic_index_in_dim(shifts, part, 1, False).reshape(-1)
    speeds = lax.dynamic_index_in_dim(speeds, part, 1, False).reshape(-1)
    sent = fluid_state.transpose(2, 0, 1, 3).reshape(planes * share, per, fields, cells)
    got = lax.all_to_all(sent, ("rad", "azi"), 0, 0, tiled=True)
    got = got.reshape(bands, blocks, per, fields, cells).transpose(0, 2, 3, 1, 4)
    cyclic = got.reshape(bands * per, fields, cycle)
    wide = jnp.concatenate([cyclic[:, :, -1:], cyclic, cyclic, cyclic[:, :, :1]], axis=2)

    def pick_row(row, start):
        return lax.dynamic_slice_in_dim(row, start, cycle + 2, axis=1)

    rimmed = jax.vmap(pick_row)(wide, jnp.where(shifts == 0, 0, cycle - shifts))
    speed = speeds[:, None, None]
    size = jnp.abs(speed)
    advected = (
        (1.0 - size) * rimmed[:, :, 1:-1]
        + (0.5 * (size + speed)) * rimmed[:, :, :-2]
        + (0.5 * (size - speed)) * rimmed[:, :, 2:]
    )
    width = cycle // share
    halves = advected.reshape(bands, per, fields, share, width).transpose(3, 0, 1, 2, 4)
    halves = swap_in_plane(halves, share).transpose(1, 0, 2, 3, 4)
    columns = halves.reshape(bands * rows * fields, width)
    solved = jnp.dot(matrix, columns, precision=lax.Precision.HIGH)
    solved = solved.reshape(bands, share, per, fields, width).transpose(1, 0, 2, 3, 4)
    solved = swap_in_plane(solved, share).reshape(share, bands, per, fields, blocks // share, cells)
    back = solved.transpose(1, 0, 4, 2, 3, 5).reshape(bands * blocks, per, fields, cells)
    back = lax.all_to_all(back, ("rad", "azi"), 0, 0, tiled=True)
    return back.reshape(planes, rows, fields, cells).transpose(1, 2, 0, 3)


def solution(mesh):
    return jax.shard_map(
        per_device,
        mesh=mesh,
        in_specs=(P("rad", None, None, "azi"), P("rad"), P("rad"), P(), P()),
        out_specs=P("rad", None, None, "azi"),
        check_vma=False,
    )
```

```python
import functools

import jax
import jax.numpy as jnp
from jax import lax
from jax.experimental import pallas as pl
from jax.experimental.pallas import tpu as pltpu
from jax.sharding import PartitionSpec as P

MESH = pl.DeviceIdType.MESH
GROUP = 8


def combined_matrix(coupling, radial_solve):
    fields, radii, _ = radial_solve.shape
    padded = jnp.pad(radial_solve, ((0, 0), (0, 0), (1, 1)))
    differences = padded[:, :, :-2] - padded[:, :, 2:]
    same = jnp.eye(fields, dtype=jnp.float32)
    solve = radial_solve.transpose(1, 0, 2)[:, :, :, None] * same[None, :, None, :]
    mixed = differences.transpose(1, 0, 2)[:, :, :, None] * coupling[None, :, None, :]
    return (solve + mixed).reshape(radii * fields, radii * fields)


def split(value):
    high = value.astype(jnp.bfloat16)
    return high, (value - high.astype(jnp.float32)).astype(jnp.bfloat16)


def mul(left, right):
    return jnp.dot(left, right, preferred_element_type=jnp.float32)


def kernel(
    bands, blocks, x, shifts, speeds, matrix, out,
    staged, landed, shared, columns, solved, arrived,
    send1, recv1, send2, recv2, send3, recv3,
):
    rows, fields, planes, cells = x.shape
    count = bands * blocks
    share = count // planes
    per = rows // share
    radii = bands * rows
    cycle = blocks * cells
    width = cycle // share
    wide = blocks // share
    band, block = lax.axis_index("rad"), lax.axis_index("azi")
    me = band * blocks + block
    part = lax.rem(block, share)
    first = me - part
    plane = me // share

    def place(device):
        return (device // blocks, lax.rem(device, blocks))

    barrier = pltpu.get_barrier_semaphore()

    @pl.loop(1, count)
    def _(step):
        pl.semaphore_signal(
            barrier, inc=1, device_id=place(lax.rem(me + step, count)), device_id_type=MESH
        )

    pl.semaphore_wait(barrier, count - 1)

    for q in range(per):
        for h in range(share):
            for g in range(planes // GROUP):
                turned = jnp.swapaxes(x[h * per + q, :, g * GROUP : (g + 1) * GROUP, :], 0, 1)
                for z in range(GROUP):
                    staged[q, (g * GROUP + z) * share + h] = turned[z]

        @pl.loop(1, count)
        def _(step):
            to = lax.rem(me + step, count)
            pltpu.make_async_remote_copy(
                src_ref=staged.at[q, to], dst_ref=landed.at[q, me],
                send_sem=send1.at[q, to], recv_sem=recv1.at[q, me],
                device_id=place(to), device_id_type=MESH,
            ).start()

        pltpu.make_async_copy(staged.at[q, me], landed.at[q, me], recv1.at[q, me]).start()

    for q in range(per):

        @pl.loop(0, count)
        def _(source):
            pltpu.make_async_copy(
                landed.at[q, source], landed.at[q, source], recv1.at[q, source]
            ).wait()

        for a in range(bands):
            row = jnp.concatenate([landed[q, a * blocks + b] for b in range(blocks)], axis=1)
            amount = shifts[a, part * per + q]
            speed = speeds[a, part * per + q]
            size = jnp.abs(speed)
            row = pltpu.roll(row, amount, 1)
            moved = (
                (1.0 - size) * row
                + (0.5 * (size + speed)) * pltpu.roll(row, 1, 1)
                + (0.5 * (size - speed)) * pltpu.roll(row, cycle - 1, 1)
            )
            k = a * rows + part * per + q
            for h in range(share):
                shared[q, a, h] = moved[:, h * width : (h + 1) * width]

                @pl.when(h != part)
                def _():
                    pltpu.make_async_remote_copy(
                        src_ref=shared.at[q, a, h], dst_ref=columns.at[k],
                        send_sem=send2.at[q, a, h], recv_sem=recv2.at[k],
                        device_id=place(first + h), device_id_type=MESH,
                    ).start()

                @pl.when(h == part)
                def _():
                    pltpu.make_async_copy(shared.at[q, a, h], columns.at[k], recv2.at[k]).start()

    @pl.loop(0, radii)
    def _(k):
        pltpu.make_async_copy(columns.at[k], columns.at[k], recv2.at[k]).wait()

    high, low = split(matrix[...])
    for c in range(wide):
        top, rest = split(
            columns[:, :, c * cells : (c + 1) * cells].reshape(radii * fields, cells)
        )
        result = mul(high, top) + (mul(high, rest) + mul(low, top))
        solved[c] = result.reshape(radii, fields, cells)
        for a in range(bands):
            owner = a * blocks + part * wide + c
            piece = solved.at[c, pl.ds(a * rows, rows)]

            @pl.when(owner != me)
            def _():
                pltpu.make_async_remote_copy(
                    src_ref=piece, dst_ref=arrived.at[plane],
                    send_sem=send3.at[c, a], recv_sem=recv3.at[plane],
                    device_id=place(owner), device_id_type=MESH,
                ).start()

            @pl.when(owner == me)
            def _():
                pltpu.make_async_copy(piece, arrived.at[plane], recv3.at[plane]).start()

    for g in range(planes // GROUP):

        @pl.loop(g * GROUP, (g + 1) * GROUP)
        def _(p):
            pltpu.make_async_copy(arrived.at[p], arrived.at[p], recv3.at[p]).wait()

        for r in range(rows):
            out[r, :, g * GROUP : (g + 1) * GROUP, :] = jnp.swapaxes(
                arrived[g * GROUP : (g + 1) * GROUP, r], 0, 1
            )

    for q in range(per):

        @pl.loop(1, count)
        def _(step):
            to = lax.rem(me + step, count)
            pltpu.make_async_copy(staged.at[q, to], staged.at[q, to], send1.at[q, to]).wait()

        for a in range(bands):
            for h in range(share):

                @pl.when(h != part)
                def _():
                    pltpu.make_async_copy(
                        shared.at[q, a, h], shared.at[q, a, h], send2.at[q, a, h]
                    ).wait()

    for c in range(wide):
        for a in range(bands):
            piece = solved.at[c, pl.ds(a * rows, rows)]

            @pl.when(a * blocks + part * wide + c != me)
            def _():
                pltpu.make_async_copy(piece, piece, send3.at[c, a]).wait()


def per_device(fluid_state, orbit_shift, residual_speed, coupling, radial_solve):
    rows, fields, planes, cells = fluid_state.shape
    bands, blocks = lax.axis_size("rad"), lax.axis_size("azi")
    count = bands * blocks
    share = count // planes
    per = rows // share
    radii = bands * rows
    width = blocks * cells // share
    wide = blocks // share
    matrix = combined_matrix(coupling, radial_solve)
    shifts = lax.all_gather(orbit_shift, "rad")
    speeds = lax.all_gather(residual_speed, "rad")
    vmem = pl.BlockSpec(memory_space=pltpu.VMEM)
    smem = pl.BlockSpec(memory_space=pltpu.SMEM)
    dma = pltpu.SemaphoreType.DMA
    return pl.pallas_call(
        functools.partial(kernel, bands, blocks),
        out_shape=jax.ShapeDtypeStruct(fluid_state.shape, jnp.float32),
        in_specs=[vmem, smem, smem, vmem],
        out_specs=vmem,
        scratch_shapes=[
            pltpu.VMEM((per, count, fields, cells), jnp.float32),
            pltpu.VMEM((per, count, fields, cells), jnp.float32),
            pltpu.VMEM((per, bands, share, fields, width), jnp.float32),
            pltpu.VMEM((radii, fields, width), jnp.float32),
            pltpu.VMEM((wide, radii, fields, cells), jnp.float32),
            pltpu.VMEM((planes, rows, fields, cells), jnp.float32),
            dma((per, count)),
            dma((per, count)),
            dma((per, bands, share)),
            dma((radii,)),
            dma((wide, bands)),
            dma((planes,)),
        ],
        compiler_params=pltpu.CompilerParams(
            collective_id=0, has_side_effects=True, vmem_limit_bytes=56 * 2**20
        ),
        cost_estimate=pl.CostEstimate(
            flops=6 * (radii * fields) ** 2 * width,
            bytes_accessed=2 * fluid_state.size * 4,
            transcendentals=0,
        ),
    )(fluid_state, shifts, speeds, matrix)


def solution(mesh):
    return jax.shard_map(
        per_device,
        mesh=mesh,
        in_specs=(P("rad", None, None, "azi"), P("rad"), P("rad"), P(), P()),
        out_specs=P("rad", None, None, "azi"),
        check_vma=False,
    )
```

```python
import functools

import jax
import jax.numpy as jnp
from jax import lax
from jax.experimental import pallas as pl
from jax.experimental.pallas import tpu as pltpu
from jax.sharding import PartitionSpec as P

MESH = pl.DeviceIdType.MESH
GROUP = 8


def fill_matrix(coupling, solve, matrix):
    fields, radii, _ = solve.shape
    shape = (radii, radii * fields)
    inner = lax.broadcasted_iota(jnp.int32, shape, 0)
    lane = lax.broadcasted_iota(jnp.int32, shape, 1)
    outer, field = lane // fields, lax.rem(lane, fields)
    zero = jnp.zeros(shape, jnp.float32)
    for f in range(fields):
        weight = zero
        for g in range(fields):
            weight = jnp.where(field == g, coupling[f, g], weight)
        spread = (
            jnp.where((inner == outer) & (field == f), 1.0, zero)
            + jnp.where(inner + 1 == outer, weight, zero)
            - jnp.where(inner == outer + 1, weight, zero)
        )
        matrix[:, f, :] = jnp.dot(
            solve[f], spread,
            precision=lax.Precision.HIGHEST, preferred_element_type=jnp.float32,
        )


def split(value):
    high = value.astype(jnp.bfloat16)
    return high, (value - high.astype(jnp.float32)).astype(jnp.bfloat16)


def mul(left, right):
    return jnp.dot(left, right, preferred_element_type=jnp.float32)


def kernel(
    bands, blocks, x, shift, speed_in, coupling, solve, arrived,
    staged, landed, shared, columns, solved, matrix, shift_all, speed_all, shifts, speeds,
    send1, recv1, send2, recv2, send3, recv3, send4, recv4, moved4,
):
    rows, fields, planes, cells = x.shape
    count = bands * blocks
    share = count // planes
    per = rows // share
    radii = bands * rows
    cycle = blocks * cells
    width = cycle // share
    wide = blocks // share
    band, block = lax.axis_index("rad"), lax.axis_index("azi")
    me = band * blocks + block
    part = lax.rem(block, share)
    first = me - part
    plane = me // share

    def place(device):
        return (device // blocks, lax.rem(device, blocks))

    barrier = pltpu.get_barrier_semaphore()

    @pl.loop(1, count)
    def _(step):
        pl.semaphore_signal(
            barrier, inc=1, device_id=place(lax.rem(me + step, count)), device_id_type=MESH
        )

    pl.semaphore_wait(barrier, count - 1)

    lane = lax.broadcasted_iota(jnp.int32, shift_all.shape[1:], 1)
    own_shift = jnp.zeros(lane.shape, jnp.int32)
    own_speed = jnp.zeros(lane.shape, jnp.float32)
    for r in range(rows):
        own_shift = jnp.where(lane == r, shift[r], own_shift)
        own_speed = jnp.where(lane == r, speed_in[r], own_speed)
    shift_all[band] = own_shift
    speed_all[band] = own_speed
    for step in range(1, bands):
        for kind, table in enumerate((shift_all, speed_all)):
            pltpu.make_async_remote_copy(
                src_ref=table.at[band], dst_ref=table.at[band],
                send_sem=send4.at[kind, step], recv_sem=recv4.at[kind, band],
                device_id=(lax.rem(band + step, bands), block), device_id_type=MESH,
            ).start()

    for q in range(per):
        for h in range(share):
            for g in range(planes // GROUP):
                turned = jnp.swapaxes(x[h * per + q, :, g * GROUP : (g + 1) * GROUP, :], 0, 1)
                for z in range(GROUP):
                    staged[q, (g * GROUP + z) * share + h] = turned[z]

        @pl.loop(1, count)
        def _(step):
            to = lax.rem(me + step, count)
            pltpu.make_async_remote_copy(
                src_ref=staged.at[q, to], dst_ref=landed.at[q, me],
                send_sem=send1.at[q, to], recv_sem=recv1.at[q, me],
                device_id=place(to), device_id_type=MESH,
            ).start()

        pltpu.make_async_copy(staged.at[q, me], landed.at[q, me], recv1.at[q, me]).start()

    fill_matrix(coupling, solve, matrix)

    for kind, table in enumerate((shift_all, speed_all)):
        for step in range(1, bands):
            other = lax.rem(band + step, bands)
            pltpu.make_async_copy(table.at[other], table.at[other], recv4.at[kind, other]).wait()
        for step in range(1, bands):
            pltpu.make_async_copy(table.at[band], table.at[band], send4.at[kind, step]).wait()
    copies = [
        pltpu.make_async_copy(shift_all, shifts, moved4.at[0]),
        pltpu.make_async_copy(speed_all, speeds, moved4.at[1]),
    ]
    for copy in copies:
        copy.start()
    for copy in copies:
        copy.wait()

    for q in range(per):

        @pl.loop(0, count)
        def _(source):
            pltpu.make_async_copy(
                landed.at[q, source], landed.at[q, source], recv1.at[q, source]
            ).wait()

        for a in range(bands):
            row = jnp.concatenate([landed[q, a * blocks + b] for b in range(blocks)], axis=1)
            amount = shifts[a, 0, part * per + q]
            speed = speeds[a, 0, part * per + q]
            size = jnp.abs(speed)
            row = pltpu.roll(row, amount, 1)
            moved = (
                (1.0 - size) * row
                + (0.5 * (size + speed)) * pltpu.roll(row, 1, 1)
                + (0.5 * (size - speed)) * pltpu.roll(row, cycle - 1, 1)
            )
            k = a * rows + part * per + q
            for h in range(share):
                shared[q, a, h] = moved[:, h * width : (h + 1) * width]

                @pl.when(h != part)
                def _():
                    pltpu.make_async_remote_copy(
                        src_ref=shared.at[q, a, h], dst_ref=columns.at[k],
                        send_sem=send2.at[q, a, h], recv_sem=recv2.at[k],
                        device_id=place(first + h), device_id_type=MESH,
                    ).start()

                @pl.when(h == part)
                def _():
                    pltpu.make_async_copy(shared.at[q, a, h], columns.at[k], recv2.at[k]).start()

    @pl.loop(0, radii)
    def _(k):
        pltpu.make_async_copy(columns.at[k], columns.at[k], recv2.at[k]).wait()

    high, low = split(matrix[...].reshape(radii * fields, radii * fields))
    for c in range(wide):
        top, rest = split(
            columns[:, :, c * cells : (c + 1) * cells].reshape(radii * fields, cells)
        )
        result = mul(high, top) + (mul(high, rest) + mul(low, top))
        solved[c] = result.reshape(radii, fields, cells)
        for a in range(bands):
            owner = a * blocks + part * wide + c
            piece = solved.at[c, pl.ds(a * rows, rows)]

            @pl.when(owner != me)
            def _():
                pltpu.make_async_remote_copy(
                    src_ref=piece, dst_ref=arrived.at[plane],
                    send_sem=send3.at[c, a], recv_sem=recv3.at[plane],
                    device_id=place(owner), device_id_type=MESH,
                ).start()

            @pl.when(owner == me)
            def _():
                pltpu.make_async_copy(piece, arrived.at[plane], recv3.at[plane]).start()

    @pl.loop(0, planes)
    def _(p):
        pltpu.make_async_copy(arrived.at[p], arrived.at[p], recv3.at[p]).wait()

    for q in range(per):

        @pl.loop(1, count)
        def _(step):
            to = lax.rem(me + step, count)
            pltpu.make_async_copy(staged.at[q, to], staged.at[q, to], send1.at[q, to]).wait()

        for a in range(bands):
            for h in range(share):

                @pl.when(h != part)
                def _():
                    pltpu.make_async_copy(
                        shared.at[q, a, h], shared.at[q, a, h], send2.at[q, a, h]
                    ).wait()

    for c in range(wide):
        for a in range(bands):
            piece = solved.at[c, pl.ds(a * rows, rows)]

            @pl.when(a * blocks + part * wide + c != me)
            def _():
                pltpu.make_async_copy(piece, piece, send3.at[c, a]).wait()


def turn_planes(planar, out):
    for r in range(out.shape[0]):
        out[r] = jnp.swapaxes(planar[:, r], 0, 1)


def per_device(fluid_state, orbit_shift, residual_speed, coupling, radial_solve):
    rows, fields, planes, cells = fluid_state.shape
    bands, blocks = lax.axis_size("rad"), lax.axis_size("azi")
    count = bands * blocks
    share = count // planes
    per = rows // share
    radii = bands * rows
    width = blocks * cells // share
    wide = blocks // share
    vmem = pl.BlockSpec(memory_space=pltpu.VMEM)
    smem = pl.BlockSpec(memory_space=pltpu.SMEM)
    dma = pltpu.SemaphoreType.DMA
    size = radii * fields
    planar = pl.pallas_call(
        functools.partial(kernel, bands, blocks),
        out_shape=jax.ShapeDtypeStruct((planes, rows, fields, cells), jnp.float32),
        in_specs=[vmem, smem, smem, smem, vmem],
        out_specs=pl.BlockSpec(memory_space=pl.ANY),
        scratch_shapes=[
            pltpu.VMEM((per, count, fields, cells), jnp.float32),
            pltpu.VMEM((per, count, fields, cells), jnp.float32),
            pltpu.VMEM((per, bands, share, fields, width), jnp.float32),
            pltpu.VMEM((radii, fields, width), jnp.float32),
            pltpu.VMEM((wide, radii, fields, cells), jnp.float32),
            pltpu.VMEM((radii, fields, size), jnp.float32),
            pltpu.VMEM((bands, 8, 128), jnp.int32),
            pltpu.VMEM((bands, 8, 128), jnp.float32),
            pltpu.SMEM((bands, 8, 128), jnp.int32),
            pltpu.SMEM((bands, 8, 128), jnp.float32),
            dma((per, count)),
            dma((per, count)),
            dma((per, bands, share)),
            dma((radii,)),
            dma((wide, bands)),
            dma((planes,)),
            dma((2, bands)),
            dma((2, bands)),
            dma((2,)),
        ],
        compiler_params=pltpu.CompilerParams(
            collective_id=0, has_side_effects=True, vmem_limit_bytes=56 * 2**20
        ),
        cost_estimate=pl.CostEstimate(
            flops=6 * (radii * fields) ** 2 * width,
            bytes_accessed=2 * fluid_state.size * 4,
            transcendentals=0,
        ),
    )(fluid_state, orbit_shift, residual_speed, coupling, radial_solve)
    some = 2
    return pl.pallas_call(
        turn_planes,
        grid=(planes // GROUP, rows // some),
        in_specs=[pl.BlockSpec((GROUP, some, fields, cells), lambda g, r: (g, r, 0, 0))],
        out_specs=pl.BlockSpec((some, fields, GROUP, cells), lambda g, r: (r, 0, g, 0)),
        out_shape=jax.ShapeDtypeStruct(fluid_state.shape, jnp.float32),
    )(planar)


def solution(mesh):
    return jax.shard_map(
        per_device,
        mesh=mesh,
        in_specs=(P("rad", None, None, "azi"), P("rad"), P("rad"), P(), P()),
        out_specs=P("rad", None, None, "azi"),
        check_vma=False,
    )
```

```python
import functools

import jax
import jax.numpy as jnp
from jax import lax
from jax.experimental import pallas as pl
from jax.experimental.pallas import tpu as pltpu
from jax.sharding import PartitionSpec as P

MESH = pl.DeviceIdType.MESH
GROUP = 8


def fill_matrix(coupling, solve, matrix):
    fields, radii, _ = solve.shape
    shape = (radii, radii * fields)
    inner = lax.broadcasted_iota(jnp.int32, shape, 0)
    lane = lax.broadcasted_iota(jnp.int32, shape, 1)
    outer, field = lane // fields, lax.rem(lane, fields)
    zero = jnp.zeros(shape, jnp.float32)
    for f in range(fields):
        weight = zero
        for g in range(fields):
            weight = jnp.where(field == g, coupling[f, g], weight)
        spread = (
            jnp.where((inner == outer) & (field == f), 1.0, zero)
            + jnp.where(inner + 1 == outer, weight, zero)
            - jnp.where(inner == outer + 1, weight, zero)
        )
        matrix[:, f, :] = jnp.dot(
            solve[f], spread,
            precision=lax.Precision.HIGHEST, preferred_element_type=jnp.float32,
        )


def split(value):
    high = value.astype(jnp.bfloat16)
    return high, (value - high.astype(jnp.float32)).astype(jnp.bfloat16)


def mul(left, right):
    return jnp.dot(left, right, preferred_element_type=jnp.float32)


def kernel(
    bands, blocks, x, shift, speed_in, coupling, solve, arrived,
    staged, landed, shared, columns, solved, matrix, shift_all, speed_all, shifts, speeds,
    send1, recv1, send2, recv2, send3, recv3, send4, recv4, moved4,
):
    rows, fields, planes, cells = x.shape
    count = bands * blocks
    share = count // planes
    per = rows // share
    radii = bands * rows
    cycle = blocks * cells
    width = cycle // share
    wide = blocks // share
    band, block = lax.axis_index("rad"), lax.axis_index("azi")
    me = band * blocks + block
    part = lax.rem(block, share)
    first = me - part
    plane = me // share

    def place(device):
        return (device // blocks, lax.rem(device, blocks))

    barrier = pltpu.get_barrier_semaphore()

    @pl.loop(1, count)
    def _(step):
        pl.semaphore_signal(
            barrier, inc=1, device_id=place(lax.rem(me + step, count)), device_id_type=MESH
        )

    pl.semaphore_wait(barrier, count - 1)

    lane = lax.broadcasted_iota(jnp.int32, shift_all.shape[1:], 1)
    own_shift = jnp.zeros(lane.shape, jnp.int32)
    own_speed = jnp.zeros(lane.shape, jnp.float32)
    for r in range(rows):
        own_shift = jnp.where(lane == r, shift[r], own_shift)
        own_speed = jnp.where(lane == r, speed_in[r], own_speed)
    shift_all[band] = own_shift
    speed_all[band] = own_speed
    for step in range(1, bands):
        for kind, table in enumerate((shift_all, speed_all)):
            pltpu.make_async_remote_copy(
                src_ref=table.at[band], dst_ref=table.at[band],
                send_sem=send4.at[kind, step], recv_sem=recv4.at[kind, band],
                device_id=(lax.rem(band + step, bands), block), device_id_type=MESH,
            ).start()

    for q in range(per):
        for h in range(share):
            for g in range(planes // GROUP):
                turned = jnp.swapaxes(x[h * per + q, :, g * GROUP : (g + 1) * GROUP, :], 0, 1)
                for z in range(GROUP):
                    staged[q, (g * GROUP + z) * share + h] = turned[z]

        @pl.loop(1, count)
        def _(step):
            to = lax.rem(me + step, count)
            pltpu.make_async_remote_copy(
                src_ref=staged.at[q, to], dst_ref=landed.at[q, me],
                send_sem=send1.at[q, to], recv_sem=recv1.at[q, me],
                device_id=place(to), device_id_type=MESH,
            ).start()

        pltpu.make_async_copy(staged.at[q, me], landed.at[q, me], recv1.at[q, me]).start()

    fill_matrix(coupling, solve, matrix)

    for kind, table in enumerate((shift_all, speed_all)):
        for step in range(1, bands):
            other = lax.rem(band + step, bands)
            pltpu.make_async_copy(table.at[other], table.at[other], recv4.at[kind, other]).wait()
        for step in range(1, bands):
            pltpu.make_async_copy(table.at[band], table.at[band], send4.at[kind, step]).wait()
    copies = [
        pltpu.make_async_copy(shift_all, shifts, moved4.at[0]),
        pltpu.make_async_copy(speed_all, speeds, moved4.at[1]),
    ]
    for copy in copies:
        copy.start()
    for copy in copies:
        copy.wait()

    for q in range(per):

        @pl.loop(0, count)
        def _(source):
            pltpu.make_async_copy(
                landed.at[q, source], landed.at[q, source], recv1.at[q, source]
            ).wait()

        for a in range(bands):
            row = jnp.concatenate([landed[q, a * blocks + b] for b in range(blocks)], axis=1)
            amount = shifts[a, 0, part * per + q]
            speed = speeds[a, 0, part * per + q]
            size = jnp.abs(speed)
            row = pltpu.roll(row, amount, 1)
            moved = (
                (1.0 - size) * row
                + (0.5 * (size + speed)) * pltpu.roll(row, 1, 1)
                + (0.5 * (size - speed)) * pltpu.roll(row, cycle - 1, 1)
            )
            k = a * rows + part * per + q
            for h in range(share):
                shared[q, a, h] = moved[:, h * width : (h + 1) * width]

                @pl.when(h != part)
                def _():
                    pltpu.make_async_remote_copy(
                        src_ref=shared.at[q, a, h], dst_ref=columns.at[k],
                        send_sem=send2.at[q, a, h], recv_sem=recv2.at[k],
                        device_id=place(first + h), device_id_type=MESH,
                    ).start()

                @pl.when(h == part)
                def _():
                    pltpu.make_async_copy(shared.at[q, a, h], columns.at[k], recv2.at[k]).start()

    @pl.loop(0, radii)
    def _(k):
        pltpu.make_async_copy(columns.at[k], columns.at[k], recv2.at[k]).wait()

    high, low = split(matrix[...].reshape(radii * fields, radii * fields))
    for c in range(wide):
        top, rest = split(
            columns[:, :, c * cells : (c + 1) * cells].reshape(radii * fields, cells)
        )
        result = mul(high, top) + (mul(high, rest) + mul(low, top))
        solved[c] = result.reshape(radii, fields, cells)
        for step in range(bands):
            a = lax.rem(band + step + 1, bands)
            owner = a * blocks + part * wide + c
            piece = solved.at[c, pl.ds(a * rows, rows)]

            @pl.when(owner != me)
            def _():
                pltpu.make_async_remote_copy(
                    src_ref=piece, dst_ref=arrived.at[plane],
                    send_sem=send3.at[c, a], recv_sem=recv3.at[plane],
                    device_id=place(owner), device_id_type=MESH,
                ).start()

            @pl.when(owner == me)
            def _():
                pltpu.make_async_copy(piece, arrived.at[plane], recv3.at[plane]).start()

    @pl.loop(0, planes)
    def _(p):
        pltpu.make_async_copy(arrived.at[p], arrived.at[p], recv3.at[p]).wait()

    for q in range(per):

        @pl.loop(1, count)
        def _(step):
            to = lax.rem(me + step, count)
            pltpu.make_async_copy(staged.at[q, to], staged.at[q, to], send1.at[q, to]).wait()

        for a in range(bands):
            for h in range(share):

                @pl.when(h != part)
                def _():
                    pltpu.make_async_copy(
                        shared.at[q, a, h], shared.at[q, a, h], send2.at[q, a, h]
                    ).wait()

    for c in range(wide):
        for a in range(bands):
            piece = solved.at[c, pl.ds(a * rows, rows)]

            @pl.when(a * blocks + part * wide + c != me)
            def _():
                pltpu.make_async_copy(piece, piece, send3.at[c, a]).wait()


def turn_planes(planar, out):
    for r in range(out.shape[0]):
        out[r] = jnp.swapaxes(planar[:, r], 0, 1)


def per_device(fluid_state, orbit_shift, residual_speed, coupling, radial_solve):
    rows, fields, planes, cells = fluid_state.shape
    bands, blocks = lax.axis_size("rad"), lax.axis_size("azi")
    count = bands * blocks
    share = count // planes
    per = rows // share
    radii = bands * rows
    width = blocks * cells // share
    wide = blocks // share
    vmem = pl.BlockSpec(memory_space=pltpu.VMEM)
    smem = pl.BlockSpec(memory_space=pltpu.SMEM)
    dma = pltpu.SemaphoreType.DMA
    size = radii * fields
    planar = pl.pallas_call(
        functools.partial(kernel, bands, blocks),
        out_shape=jax.ShapeDtypeStruct((planes, rows, fields, cells), jnp.float32),
        in_specs=[vmem, smem, smem, smem, vmem],
        out_specs=pl.BlockSpec(memory_space=pl.ANY),
        scratch_shapes=[
            pltpu.VMEM((per, count, fields, cells), jnp.float32),
            pltpu.VMEM((per, count, fields, cells), jnp.float32),
            pltpu.VMEM((per, bands, share, fields, width), jnp.float32),
            pltpu.VMEM((radii, fields, width), jnp.float32),
            pltpu.VMEM((wide, radii, fields, cells), jnp.float32),
            pltpu.VMEM((radii, fields, size), jnp.float32),
            pltpu.VMEM((bands, 8, 128), jnp.int32),
            pltpu.VMEM((bands, 8, 128), jnp.float32),
            pltpu.SMEM((bands, 8, 128), jnp.int32),
            pltpu.SMEM((bands, 8, 128), jnp.float32),
            dma((per, count)),
            dma((per, count)),
            dma((per, bands, share)),
            dma((radii,)),
            dma((wide, bands)),
            dma((planes,)),
            dma((2, bands)),
            dma((2, bands)),
            dma((2,)),
        ],
        compiler_params=pltpu.CompilerParams(
            collective_id=0, has_side_effects=True, vmem_limit_bytes=56 * 2**20
        ),
        cost_estimate=pl.CostEstimate(
            flops=6 * (radii * fields) ** 2 * width,
            bytes_accessed=2 * fluid_state.size * 4,
            transcendentals=0,
        ),
    )(fluid_state, orbit_shift, residual_speed, coupling, radial_solve)
    some = 2
    return pl.pallas_call(
        turn_planes,
        grid=(planes // GROUP, rows // some),
        in_specs=[pl.BlockSpec((GROUP, some, fields, cells), lambda g, r: (g, r, 0, 0))],
        out_specs=pl.BlockSpec((some, fields, GROUP, cells), lambda g, r: (r, 0, g, 0)),
        out_shape=jax.ShapeDtypeStruct(fluid_state.shape, jnp.float32),
    )(planar)


def solution(mesh):
    return jax.shard_map(
        per_device,
        mesh=mesh,
        in_specs=(P("rad", None, None, "azi"), P("rad"), P("rad"), P(), P()),
        out_specs=P("rad", None, None, "azi"),
        check_vma=False,
    )
```
